32 devices in a mesh: dp: 16 (over z, y, core), text: 2 (over x).
Axes of the slice: x: 2, y: 2, z: 4, core: 2. Of those that a mesh axis runs over, the one named last changes fastest.
Arguments:
- tokens_in: bfloat16 [8192, 2048], P(('dp', 'text')), may hold values from -6 to 6
- mask_flags: int32 [8192], P(('dp', 'text')), may hold values from 0 to 1, as said below
- text_states: bfloat16 [32, 128, 2048], P('dp', 'text'), may hold values from -6 to 6
- mask_embed: bfloat16 [2048], P(('dp', 'text')), may hold values from -6 to 6
- gain_attn: bfloat16 [2048], P(('dp', 'text')), may hold values from 0.25 to 1.75
- bias_attn: bfloat16 [2048], P(('dp', 'text')), may hold values from -3 to 3
- attn_query: bfloat16 [2048, 2048], P(('dp', 'text')), may hold values from -0.125 to 0.125
- attn_key: bfloat16 [2048, 2048], P(('dp', 'text')), may hold values from -0.125 to 0.125
- attn_value: bfloat16 [2048, 2048], P(('dp', 'text')), may hold values from -0.125 to 0.125
- attn_out: bfloat16 [2048, 2048], P(('dp', 'text')), may hold values from -2 to 2
- gain_cross: bfloat16 [2048], P(('dp', 'text')), may hold values from 0.25 to 1.75
- bias_cross: bfloat16 [2048], P(('dp', 'text')), may hold values from -3 to 3
- cross_query: bfloat16 [2048, 2048], P(('dp', 'text')), may hold values from -0.125 to 0.125
- cross_key: bfloat16 [2048, 2048], P(('dp', 'text')), may hold values from -0.125 to 0.125
- cross_value: bfloat16 [2048, 2048], P(('dp', 'text')), may hold values from -0.125 to 0.125
- cross_out: bfloat16 [2048, 2048], P(('dp', 'text')), may hold values from -1.5 to 1.5
- gain_mlp: bfloat16 [2048], P(('dp', 'text')), may hold values from 0.25 to 1.75
- bias_mlp: bfloat16 [2048], P(('dp', 'text')), may hold values from -3 to 3
- mlp_in: bfloat16 [2048, 8192], P(('dp', 'text')), may hold values from -0.125 to 0.125
- mlp_out: bfloat16 [8192, 2048], P(('dp', 'text')), may hold values from -0.0625 to 0.0625
- out_grad: bfloat16 [8192, 2048], P(('dp', 'text')), may hold values from -6 to 6
Outputs:
- output: bfloat16 [8192, 2048], P(('dp', 'text'))
- tokens_grad: float32 [8192, 2048], P(('dp', 'text'))
- text_grad: float32 [32, 128, 2048], P('dp', 'text')
- mask_embed_grad: float32 [2048], P(('dp', 'text'))
- gain_attn_grad: float32 [2048], P(('dp', 'text'))
- bias_attn_grad: float32 [2048], P(('dp', 'text'))
- attn_query_grad: float32 [2048, 2048], P(('dp', 'text'))
- attn_key_grad: float32 [2048, 2048], P(('dp', 'text'))
- attn_value_grad: float32 [2048, 2048], P(('dp', 'text'))
- attn_out_grad: float32 [2048, 2048], P(('dp', 'text'))
- gain_cross_grad: float32 [2048], P(('dp', 'text'))
- bias_cross_grad: float32 [2048], P(('dp', 'text'))
- cross_query_grad: float32 [2048, 2048], P(('dp', 'text'))
- cross_key_grad: float32 [2048, 2048], P(('dp', 'text'))
- cross_value_grad: float32 [2048, 2048], P(('dp', 'text'))
- cross_out_grad: float32 [2048, 2048], P(('dp', 'text'))
- gain_mlp_grad: float32 [2048], P(('dp', 'text'))
- bias_mlp_grad: float32 [2048], P(('dp', 'text'))
- mlp_in_grad: float32 [2048, 8192], P(('dp', 'text'))
- mlp_out_grad: float32 [8192, 2048], P(('dp', 'text'))
The draws below stay inside these ranges and needn't reach their ends.
Inputs may be any that keep to these rules, and one draw needn't show every extreme that they name: `mask_flags`: for each image a masking ratio is drawn from a cosine plan, and a number of its 256 tokens between 1 and 256, set by that ratio, is flagged at positions drawn uniformly.
All inputs are finite; a program needn't handle non-finite values.
Results may differ from the reference program's by a relative error of at most 0.025.
Values may be sent and summed in bfloat16 or wider, within the bound.
No kernel may reach another device: no remote copies, remote signals or barrier semaphores. Data moves between devices by JAX's collectives and lax.ppermute only.
A program may use at most 576 MiB of HBM per device.

```python
import math
import jax
import jax.numpy as jnp
import numpy as np
from jax import lax

D = 2048
H = 16
DH = 128
FF = 8192
L = 256
CTX = 128
IMAGES = 32
TOKENS = 8192


def draw_mask_flags(key, part):
    key = jax.random.fold_in(key, 11)
    images = TOKENS // L
    table = np.maximum(1, np.minimum(L, np.ceil(L * np.cos(0.5 * np.pi * np.arange(1024) / 1024.0) - 1e-09))).astype(np.int32)
    count_key, order_key = jax.random.split(key)
    picks = jax.random.randint(count_key, (images,), 0, 1024)
    counts = jnp.asarray(table)[picks]
    order_keys = jax.random.split(order_key, images)
    ranks = jax.vmap(lambda subkey: jax.random.permutation(subkey, L))(order_keys)
    return (ranks < counts[:, None]).astype(jnp.int32).reshape(TOKENS)


def block_scale(key, shape, cuts, least, largest):
    def one(position, blocks):
        steps = jax.random.uniform(jax.random.fold_in(jax.random.fold_in(key, 6), position), (blocks,), jnp.float32, least / len(cuts), largest / len(cuts))
        return jnp.repeat(jnp.exp(steps), shape[position] // blocks).reshape((-1,) + (1,) * (len(shape) - position - 1))

    level = one(*cuts[0])
    for cut in cuts[1:]:
        level = level * one(*cut)
    return level


def scatter_about(key, dims, width, limit, shards=(), held_as=jnp.bfloat16):
    factor_of = block_scale(key, dims, shards, -0.22, 0.18) if shards else 1.0
    drawn = jax.random.normal(key, dims, jnp.float32) * width * factor_of
    return jnp.minimum(jnp.maximum(drawn, -limit), limit).astype(held_as)


def setup_inputs(seed: int = 0) -> dict:
    streams_of = jax.random.split(jax.random.key(seed), 22)
    tokens_in = scatter_about(streams_of[0], (TOKENS, D), 1.0, 6.0, ((0, 32),))
    mask_flags = draw_mask_flags(jax.random.fold_in(streams_of[21], 71), 0)
    text_states = scatter_about(streams_of[2], (IMAGES, CTX, D), 1.0, 6.0, ((0, 16), (1, 2)))
    mask_embed = scatter_about(streams_of[3], (D,), 1.0, 6.0, ((0, 32),))
    gain_attn = jnp.clip(1.0 + 0.15 * jax.random.normal(streams_of[4], (D,), jnp.float32), 0.25, 1.75).astype(jnp.bfloat16)
    bias_attn = scatter_about(streams_of[5], (D,), 0.3, 3.0, ((0, 32),))
    attn_query = scatter_about(streams_of[6], (D, D), D ** -0.5, 0.125, ((0, 32),))
    attn_key = scatter_about(streams_of[7], (D, D), D ** -0.5, 0.125, ((0, 32),))
    attn_value = scatter_about(streams_of[8], (D, D), D ** -0.5, 0.125, ((0, 32),))
    attn_out = scatter_about(streams_of[9], (D, D), (D // L) ** -0.5, 2.0, ((0, 32),))
    gain_cross = jnp.clip(1.0 + 0.15 * jax.random.normal(streams_of[10], (D,), jnp.float32), 0.25, 1.75).astype(jnp.bfloat16)
    bias_cross = scatter_about(streams_of[11], (D,), 0.3, 3.0, ((0, 32),))
    cross_query = scatter_about(streams_of[12], (D, D), D ** -0.5, 0.125, ((0, 32),))
    cross_key = scatter_about(streams_of[13], (D, D), D ** -0.5, 0.125, ((0, 32),))
    cross_value = scatter_about(streams_of[14], (D, D), D ** -0.5, 0.125, ((0, 32),))
    cross_out = scatter_about(streams_of[15], (D, D), (D // CTX) ** -0.5, 1.5, ((0, 32),))
    gain_mlp = jnp.clip(1.0 + 0.15 * jax.random.normal(streams_of[16], (D,), jnp.float32), 0.25, 1.75).astype(jnp.bfloat16)
    bias_mlp = scatter_about(streams_of[17], (D,), 0.3, 3.0, ((0, 32),))
    mlp_in = scatter_about(streams_of[18], (D, FF), D ** -0.5, 0.125, ((0, 32),))
    mlp_out = scatter_about(streams_of[19], (FF, D), FF ** -0.5, 0.0625, ((0, 32),))
    out_grad = scatter_about(streams_of[20], (TOKENS, D), 1.0, 6.0, ((0, 32),))
    return dict(tokens_in=tokens_in, mask_flags=mask_flags, text_states=text_states, mask_embed=mask_embed, gain_attn=gain_attn, bias_attn=bias_attn, attn_query=attn_query, attn_key=attn_key, attn_value=attn_value, attn_out=attn_out, gain_cross=gain_cross, bias_cross=bias_cross, cross_query=cross_query, cross_key=cross_key, cross_value=cross_value, cross_out=cross_out, gain_mlp=gain_mlp, bias_mlp=bias_mlp, mlp_in=mlp_in, mlp_out=mlp_out, out_grad=out_grad)


@jax.custom_vjp
def low(v):
    return lax.optimization_barrier(v.astype(jnp.bfloat16)).astype(jnp.float32)

@jax.custom_vjp
def low_back(v):
    return v

def low_keep(v):
    return (low(v), None)

def low_pass(kept, grad):
    return (grad,)

def back_keep(v):
    return (v, None)

def back_low(kept, grad):
    return (low(grad),)
low.defvjp(low_keep, low_pass)
low_back.defvjp(back_keep, back_low)
epsilon = 1e-06
highest = lax.Precision.HIGHEST

def layer_norm(rows, gain, bias):
    mean = lax.optimization_barrier(jnp.mean(rows, axis=-1, keepdims=True))
    centered = rows - mean
    inverse = lax.rsqrt(lax.optimization_barrier(jnp.mean(centered * centered, axis=-1, keepdims=True)) + epsilon)
    return centered * inverse * gain + bias

def project(rows, matrix):
    return jnp.einsum('rd,de->re', rows, matrix, precision=highest)

def attend(queries, keys, values):
    head_scale = DH ** (-0.5)
    scores = low_back(jnp.einsum('glhe,gche->ghlc', queries, keys, precision=highest) * head_scale)
    weights = low(jax.nn.softmax(scores, axis=-1))
    return low(low_back(jnp.einsum('ghlc,gche->glhe', weights, values, precision=highest)))

def block_forward(params, tokens, flags, text):
    mask_embed, gain_attn, bias_attn, attn_query, attn_key, attn_value, attn_out, gain_cross, bias_cross, cross_query, cross_key, cross_value, cross_out, gain_mlp, bias_mlp, mlp_in, mlp_out = params
    images = text.shape[0]
    start = jnp.where(flags[:, None] == 1, mask_embed[None, :], tokens)
    normed = low(layer_norm(start, gain_attn, bias_attn))
    queries = low(low_back(project(normed, attn_query))).reshape(images, L, H, DH)
    keys = low(low_back(project(normed, attn_key))).reshape(images, L, H, DH)
    values = low(low_back(project(normed, attn_value))).reshape(images, L, H, DH)
    mixed = attend(queries, keys, values).reshape(images * L, D)
    first = start + low_back(project(mixed, attn_out))
    cross_normed = low(layer_norm(first, gain_cross, bias_cross))
    cross_queries = low(low_back(project(cross_normed, cross_query))).reshape(images, L, H, DH)
    text_rows = text.reshape(images * CTX, D)
    text_keys = low(low_back(project(text_rows, cross_key))).reshape(images, CTX, H, DH)
    text_values = low(low_back(project(text_rows, cross_value))).reshape(images, CTX, H, DH)
    cross_mixed = attend(cross_queries, text_keys, text_values).reshape(images * L, D)
    second = first + low_back(project(cross_mixed, cross_out))
    mlp_normed = low(layer_norm(second, gain_mlp, bias_mlp))
    hidden_pre = low_back(project(mlp_normed, mlp_in))
    activated = low(jax.nn.gelu(hidden_pre, approximate=False))
    return second + low_back(project(activated, mlp_out))

def reference(tokens_in, mask_flags, text_states, mask_embed, gain_attn, bias_attn, attn_query, attn_key, attn_value, attn_out, gain_cross, bias_cross, cross_query, cross_key, cross_value, cross_out, gain_mlp, bias_mlp, mlp_in, mlp_out, out_grad):
    group_size = math.gcd(IMAGES, 16)
    groups = IMAGES // group_size
    params = tuple((item.astype(jnp.float32) for item in (mask_embed, gain_attn, bias_attn, attn_query, attn_key, attn_value, attn_out, gain_cross, bias_cross, cross_query, cross_key, cross_value, cross_out, gain_mlp, bias_mlp, mlp_in, mlp_out)))
    tokens = tokens_in.astype(jnp.float32).reshape(groups, group_size * L, D)
    flags = mask_flags.reshape(groups, group_size * L)
    text = text_states.astype(jnp.float32).reshape(groups, group_size, CTX, D)
    checked = jax.checkpoint(block_forward)

    def whole(params, tokens, text):

        def one_group(carry, pieces):
            return (carry, checked(params, pieces[0], pieces[1], pieces[2]))
        unused, outs = lax.scan(one_group, jnp.zeros((), jnp.float32), (tokens, flags, text))
        return outs
    result, pullback = jax.vjp(whole, params, tokens, text)
    cotangent = out_grad.astype(jnp.float32).reshape(groups, group_size * L, D)
    params_grad, tokens_grad, text_grad = pullback(cotangent)
    return (result.reshape(TOKENS, D).astype(jnp.bfloat16), tokens_grad.reshape(TOKENS, D), text_grad.reshape(IMAGES, CTX, D), params_grad[0], params_grad[1], params_grad[2], params_grad[3], params_grad[4], params_grad[5], params_grad[6], params_grad[7], params_grad[8], params_grad[9], params_grad[10], params_grad[11], params_grad[12], params_grad[13], params_grad[14], params_grad[15], params_grad[16])
```

```python
import functools

import jax
import jax.numpy as jnp
from jax import lax
from jax.experimental import pallas as pl
from jax.experimental.pallas import tpu as pltpu
from jax.sharding import PartitionSpec as P

DH = 128
L = 256
AXES = ("g", "core", "x")
F32 = jnp.float32
BF16 = jnp.bfloat16
epsilon = 1e-06


def normalize(rows):
    mean = jnp.mean(rows, axis=-1, keepdims=True)
    centered = rows - mean
    inverse = lax.rsqrt(jnp.mean(centered * centered, axis=-1, keepdims=True) + epsilon)
    return (centered * inverse, inverse)


def norm_backward(grad_out, unit_rows, inverse, gain):
    scaled = grad_out * gain
    mean_grad = jnp.mean(scaled, axis=-1, keepdims=True)
    mean_mixed = jnp.mean(scaled * unit_rows, axis=-1, keepdims=True)
    rows_grad = inverse * (scaled - mean_grad - unit_rows * mean_mixed)
    return (rows_grad, jnp.sum(grad_out * unit_rows, axis=0), jnp.sum(grad_out, axis=0))


def product(left, right):
    return jnp.dot(left, right, preferred_element_type=F32)


def outer_grad(left, right):
    return lax.dot_general(left, right, (((0,), (0,)), ((), ())), preferred_element_type=F32)


def back_project(left, right):
    return lax.dot_general(left, right, (((1,), (1,)), ((), ())), preferred_element_type=F32)


def forward_head(query, key, value, scale):
    scores = back_project(query, key) * scale
    exps = jnp.exp(scores - jnp.max(scores, axis=1, keepdims=True))
    weights = exps * (1.0 / jnp.sum(exps, axis=1, keepdims=True))
    return product(weights.astype(BF16), value).astype(BF16)


def backward_head(query, key, value, mixed_grad, scale):
    scores = back_project(key, query) * scale
    exps = jnp.exp(scores - jnp.max(scores, axis=0, keepdims=True))
    weights = exps * (1.0 / jnp.sum(exps, axis=0, keepdims=True))
    value_grad = product(weights.astype(BF16), mixed_grad)
    weight_grad = back_project(value, mixed_grad)
    delta = jnp.sum(weights * weight_grad, axis=0, keepdims=True)
    score_grad = (weights * (weight_grad - delta)).astype(BF16)
    query_grad = outer_grad(score_grad, key) * scale
    key_grad = product(score_grad, query) * scale
    return (query_grad.astype(BF16), key_grad.astype(BF16), value_grad.astype(BF16))


def self_forward_kernel(width, scale, qkv, mixed):
    for low in range(0, width, DH):
        at = [slice(part * width + low, part * width + low + DH) for part in range(3)]
        mixed[:, at[0]] = forward_head(qkv[:, at[0]], qkv[:, at[1]], qkv[:, at[2]], scale)


def self_backward_kernel(width, scale, qkv, mixed_grad, grads):
    for low in range(0, width, DH):
        at = [slice(part * width + low, part * width + low + DH) for part in range(3)]
        terms = backward_head(
            qkv[:, at[0]], qkv[:, at[1]], qkv[:, at[2]], mixed_grad[:, at[0]], scale
        )
        for part in range(3):
            grads[:, at[part]] = terms[part]


def cross_forward_kernel(width, scale, queries, text, mixed):
    for low in range(0, width, DH):
        at = [slice(part * width + low, part * width + low + DH) for part in range(2)]
        mixed[:, at[0]] = forward_head(queries[:, at[0]], text[:, at[0]], text[:, at[1]], scale)


def cross_backward_kernel(width, scale, queries, text, mixed_grad, query_grads, text_grads):
    for low in range(0, width, DH):
        at = [slice(part * width + low, part * width + low + DH) for part in range(2)]
        terms = backward_head(
            queries[:, at[0]], text[:, at[0]], text[:, at[1]], mixed_grad[:, at[0]], scale
        )
        query_grads[:, at[0]] = terms[0]
        text_grads[:, at[0]] = terms[1]
        text_grads[:, at[1]] = terms[2]


def by_image(kernel, args, blocks, shapes, out_blocks, flops, skip=0):
    images = shapes[0][0] // out_blocks[0][0]
    offsets = [0 if arg.shape[0] // block[0] == images else skip for arg, block in zip(args, blocks)]
    total = sum(images * block[0] * block[1] * 2 for block in (*blocks, *out_blocks))
    return pl.pallas_call(
        kernel,
        grid=(images,),
        in_specs=[
            pl.BlockSpec(block, functools.partial(lambda off, i: (i + off, 0), off))
            for block, off in zip(blocks, offsets)
        ],
        out_specs=[pl.BlockSpec(block, lambda i: (i, 0)) for block in out_blocks],
        out_shape=[jax.ShapeDtypeStruct(shape, BF16) for shape in shapes],
        compiler_params=pltpu.CompilerParams(vmem_limit_bytes=32 * 1024 * 1024),
        cost_estimate=pl.CostEstimate(
            flops=flops, bytes_accessed=total, transcendentals=flops // 512
        ),
    )(*args)


def head_start(piece, rank):
    return DH * (4 * piece + 2 * (rank & 1) + (rank >> 1))


def hidden_start(size, piece, rank):
    return size * (4 * piece + rank)


def lanes_at(start, size):
    return pl.ds(pl.multiple_of(start, 128), size)


def cut_kernel(start, pieces, size, rank_ref, *refs):
    weights, (own, to_x, to_core) = refs[:-3], refs[-3:]
    for rel, out in ((0, own), (1, to_x.at[0]), (3, to_x.at[1]), (2, to_core)):
        rank = rank_ref[0] ^ rel
        for k, weight in enumerate(weights):
            for piece in range(pieces):
                column = (k * pieces + piece) * size
                out[:, column : column + size] = weight[:, lanes_at(start(piece, rank), size)]


def join_kernel(start, pieces, size, rank_ref, own, from_x, from_core, *outs):
    for rel, source in ((0, own), (1, from_x.at[0]), (2, from_core.at[0]), (3, from_core.at[1])):
        rank = rank_ref[0] ^ rel
        for k, out in enumerate(outs):
            for piece in range(pieces):
                column = (k * pieces + piece) * size
                value = source[:, column : column + size].astype(F32)
                out[:, lanes_at(start(piece, rank), size)] = value


def order_kernel(rank_ref, own, from_x, from_core, *refs):
    extra, (first, second) = refs[:-2], refs[-2:]
    rows, columns = own.shape
    lane = first.shape[1]
    for rel, source in ((0, own), (1, from_x.at[0]), (2, from_core.at[0]), (3, from_core.at[1])):
        at = pl.ds(pl.multiple_of((rank_ref[0] ^ rel) * rows, rows), rows)
        first[at, :] = source[:, :lane]
        second[at, : columns - lane] = source[:, lane:]
    for weight in extra:
        size = weight.shape[1] // 4
        for part in range(4):
            piece = weight[:, part * size : (part + 1) * size]
            second[part * rows : (part + 1) * rows, columns - lane :] = piece


def assemble_kernel(plan, count, places_ref, *refs):
    sources, outs, sems = refs[:count], refs[count:-1], refs[-1]
    copies = []
    for piece, place, moves in plan:
        for rows, columns, out, to_rows, to_columns in moves:
            copies.append(
                pltpu.make_async_copy(
                    sources[piece].at[pl.ds(*rows), pl.ds(*columns)],
                    outs[out].at[places_ref[place], pl.ds(*to_rows), pl.ds(*to_columns)],
                    sems.at[len(copies)],
                )
            )
            copies[-1].start()
    for copy in copies:
        copy.wait()


def whole_call(kernel, rank, args, shapes, dtype):
    moved = 2 * sum(arg.size * arg.dtype.itemsize for arg in args)
    return pl.pallas_call(
        kernel,
        in_specs=[pl.BlockSpec(memory_space=pltpu.SMEM)]
        + [pl.BlockSpec(memory_space=pltpu.VMEM)] * len(args),
        out_specs=[pl.BlockSpec(memory_space=pltpu.VMEM)] * len(shapes),
        out_shape=[jax.ShapeDtypeStruct(shape, dtype) for shape in shapes],
        compiler_params=pltpu.CompilerParams(vmem_limit_bytes=24 * 1024 * 1024),
        cost_estimate=pl.CostEstimate(flops=0, bytes_accessed=moved, transcendentals=0),
    )(rank, *args)


def assemble(plan, places, pieces, shapes):
    count = sum(len(moves) for piece, place, moves in plan)
    moved = 2 * sum(piece.size * piece.dtype.itemsize for piece in pieces)
    return pl.pallas_call(
        functools.partial(assemble_kernel, plan, len(pieces)),
        in_specs=[pl.BlockSpec(memory_space=pltpu.SMEM)]
        + [pl.BlockSpec(memory_space=pltpu.VMEM)] * len(pieces),
        out_specs=[pl.BlockSpec(memory_space=pl.ANY)] * len(shapes),
        out_shape=[jax.ShapeDtypeStruct(shape, BF16) for shape in shapes],
        scratch_shapes=[pltpu.SemaphoreType.DMA((count,))],
        compiler_params=pltpu.CompilerParams(vmem_limit_bytes=24 * 1024 * 1024),
        cost_estimate=pl.CostEstimate(flops=0, bytes_accessed=moved, transcendentals=0),
    )(places, *pieces)


def on_device(
    n_g,
    tokens_in,
    mask_flags,
    text_states,
    mask_embed,
    gain_attn,
    bias_attn,
    attn_query,
    attn_key,
    attn_value,
    attn_out,
    gain_cross,
    bias_cross,
    cross_query,
    cross_key,
    cross_value,
    cross_out,
    gain_mlp,
    bias_mlp,
    mlp_in,
    mlp_out,
    out_grad,
):
    n = n_g * 4
    half_ring = n_g // 2
    rows, width = tokens_in.shape
    own_rows = attn_query.shape[0]
    hidden = mlp_in.shape[1]
    heads = width // DH
    rank_heads = heads // 4
    rank_width = rank_heads * DH
    parts = n // heads
    ctx = 2 * text_states.shape[1]
    images = rows // L
    scale = DH ** (-0.5)

    g = lax.axis_index("g")
    core = lax.axis_index("core")
    x = lax.axis_index("x")

    order = list(range(0, n_g, 2)) + list(range(n_g - 1, 0, -2))
    ahead = {order[p]: order[(p + 1) % n_g] for p in range(n_g)}
    swap_x = [(i, i ^ 1) for i in range(n)]
    swap_core = [(i, i ^ 2) for i in range(n)]
    go_next = [(i, ahead[i // 4] * 4 + i % 4) for i in range(n)]
    go_prev = [(j, i) for i, j in go_next]
    place = jnp.where((g & 1) == 0, g >> 1, n_g - 1 - (g >> 1))

    def g_at(offset):
        p = place + (offset % n_g)
        p = jnp.where(p >= n_g, p - n_g, p)
        return jnp.where(p < half_ring, 2 * p, 2 * (n_g - 1 - p) + 1)

    def send(value, pairs):
        return lax.ppermute(value, AXES, pairs)

    token = mask_flags

    def pin(*values):
        nonlocal token
        values, token = lax.optimization_barrier((values, token))
        return values if len(values) > 1 else values[0]

    def flip(blocks):
        blocks = [jnp.where(x == 1, blocks[k ^ 1], blocks[k]) for k in range(4)]
        return [jnp.where(core == 1, blocks[k ^ 2], blocks[k]) for k in range(4)]

    me = g * 4 + core * 2 + x
    rank = jnp.reshape(core * 2 + x, (1,)).astype(jnp.int32)
    lane = width // 2
    hidden_rows = mlp_out.shape[0]
    head_cut = (head_start, rank_heads, DH)
    hidden_cut = (functools.partial(hidden_start, hidden_rows), n_g, hidden_rows)

    def pieces_of(cut, size):
        return [[int(cut[0](piece, to)) for piece in range(cut[1])] for to in range(4)]

    def cut_columns(weights, cut):
        start, pieces, size = cut
        if size % 128 == 0:
            shape = (own_rows, len(weights) * pieces * size)
            kernel = functools.partial(cut_kernel, start, pieces, size)
            return whole_call(kernel, pin(rank), weights, [shape, (2,) + shape, shape], BF16)
        rel = flip(
            [
                jnp.concatenate(
                    [weight[:, low : low + size] for weight in weights for low in lows], axis=1
                )
                for lows in pieces_of(cut, size)
            ]
        )
        return (rel[0], jnp.stack([rel[1], rel[3]]), rel[2])

    def join_columns(own, from_x, from_core, cut, count):
        start, pieces, size = cut
        if size % 128 == 0:
            shape = (own_rows, 4 * pieces * size)
            kernel = functools.partial(join_kernel, start, pieces, size)
            return whole_call(kernel, rank, [own, from_x, from_core], [shape] * count, F32)
        blocks = flip([own, from_x[0], from_core[0], from_core[1]])
        outs = []
        for k in range(count):
            found = sorted(
                (low, to, k * pieces + piece)
                for to, lows in enumerate(pieces_of(cut, size))
                for piece, low in enumerate(lows)
            )
            parts = [blocks[to][:, at * size : (at + 1) * size] for low, to, at in found]
            outs.append(jnp.concatenate(parts, axis=1).astype(F32))
        return outs

    def exchange_x(blocks):
        own, to_x, to_core = blocks
        return (own, to_core, send(to_x, swap_x))

    def exchange_core(state):
        own, to_core, from_x = state
        from_x = pin(from_x)
        return (own, from_x, send(jnp.stack([to_core, from_x[1]]), swap_core))

    def exchange_end(state):
        own, from_x, from_core = state
        return (own, from_x, pin(from_core))

    def in_order(state, *extra):
        shapes = [(4 * own_rows, lane)] * 2
        return whole_call(order_kernel, rank, list(exchange_end(state)) + list(extra), shapes, BF16)

    pieces = {}
    lanes_left = {"self": 2, "cross": 2, "in": 2, "down": 2}
    sums = {}
    places = jnp.stack([g_at(offset) for offset in range(n_g)]).astype(jnp.int32)

    def gather_task(name, side, block):
        found = pieces.setdefault((name, side), [])
        found.append((block, 0, 0))
        clock = counter = block
        half = block.shape[0] // 2
        for step in range(1, half_ring + 1):
            if step == half_ring:
                clock, counter = clock[:half], counter[half:]
            clock, counter = yield [(clock, go_next), (counter, go_prev)]
            found.append((clock, -step % n_g, 0))
            found.append((counter, step, half if step == half_ring else 0))
        lanes_left[name] -= 1

    def reduce_task(name, value, column):
        rows_of = value.shape[1]

        def mine(offset):
            return lax.dynamic_slice(value, (g_at(offset), 0, column), (1, rows_of, lane))[0]

        block = mine(half_ring)
        half = rows_of // 2
        clock, counter = block[:half], block[half:]
        for step in range(half_ring - 1, -1, -1):
            clock, counter = yield [(clock, go_next), (counter, go_prev)]
            clock, counter = clock.astype(F32), counter.astype(F32)
            up, down = mine(step).astype(F32), mine(-step).astype(F32)
            if step == half_ring - 1:
                clock = jnp.concatenate([up[:half] + clock, up[half:]]).astype(BF16)
                counter = jnp.concatenate([down[:half], down[half:] + counter]).astype(BF16)
            elif step:
                clock, counter = (up + clock).astype(BF16), (down + counter).astype(BF16)
        sums[name] = up + clock + counter

    waiting = [[], []]
    flying = [None, None]
    turn = 0

    def launch(side):
        if waiting[side] and flying[side] is None:
            task, rounds, sends = waiting[side].pop(0)
            if sends is None:
                sends = next(task)
            else:
                values = pin(*[value for value, pairs in sends])
                values = values if len(sends) > 1 else [values]
                sends = [(value, pairs) for value, (old, pairs) in zip(values, sends)]
            flying[side] = (task, rounds, [send(*item) for item in sends])

    def enter(side, task, rounds=0):
        waiting[side].append((task, rounds, None))
        launch(side)

    def visit(side):
        if flying[side] is None:
            return
        task, rounds, flight = flying[side]
        values = pin(*flight)
        flying[side] = None
        try:
            sends = task.send(values)
            if rounds == 1:
                waiting[side].append((task, 0, sends))
            else:
                flying[side] = (task, rounds - 1, [send(*item) for item in sends])
        except StopIteration:
            pass
        launch(side)

    def ring(steps):
        nonlocal turn
        for unused in range(steps):
            visit(turn)
            turn ^= 1

    def settle(name, shapes, moves):
        while lanes_left[name]:
            ring(1)
        plan = []
        values = []
        for side in range(2):
            for value, place, low in pieces[name, side]:
                high = low + value.shape[0]
                inside = []
                for (row, size), columns, out, (to_row, unused), to_columns in moves[side]:
                    first, last = max(row, low), min(row + size, high)
                    if first < last:
                        to = (to_row + first - row, last - first)
                        inside.append(((first - low, last - first), columns, out, to, to_columns))
                plan.append((len(values), place, inside))
                values.append(value)
        shapes = [(n_g,) + shape for shape in shapes]
        outs = assemble(plan, places, values, shapes)
        return [out.reshape(n_g * out.shape[1], out.shape[2]) for out in outs]

    def summed(name):
        while name not in sums:
            ring(1)
        return sums[name]

    def join_near(value, from_core):
        return jnp.concatenate([value, from_core])

    def send_far(far):
        from_diagonal = pin(send(far[1], swap_core))
        across = pin((far[0].astype(F32) + from_diagonal.astype(F32)).astype(BF16))
        return send(across, swap_x)

    def add_near(near, from_core, from_x):
        return near + from_x.astype(F32) + from_core.astype(F32)

    def pair(value):
        return value.reshape((2, value.shape[0] // 2) + value.shape[1:])

    to_ranks = []
    for i in range(n):
        head, part = i // parts, i % parts
        to_ranks.append((i, ((head // 4) * parts + part) * 4 + (head % 2) * 2 + (head // 2) % 2))
    from_ranks = [(j, i) for i, j in to_ranks]

    block_rows = 4 * own_rows
    block = (0, block_rows)
    stacked = [
        ((part * own_rows, own_rows), (rank_width, rank_width), 1, (0, own_rows), (part * rank_width, rank_width))
        for part in range(4)
    ]

    for side in range(2):
        enter(side, gather_task("down", side, mlp_out[:, side * lane : (side + 1) * lane]), 1)
    qkv_state = exchange_x(cut_columns([attn_query, attn_key, attn_value], head_cut))
    vectors = jnp.stack(
        [
            mask_embed,
            gain_attn,
            bias_attn,
            gain_cross,
            bias_cross,
            gain_mlp,
            bias_mlp,
            jnp.zeros_like(bias_mlp),
        ]
    ).astype(F32)[None]

    bits = n.bit_length() - 1
    later = [None, None]
    out_block = send(attn_out, to_ranks)
    for bit in range(bits):
        other = pin(send(vectors, [(i, i ^ (1 << bit)) for i in range(n)]))
        upper = (me >> bit) & 1 == 1
        vectors = jnp.concatenate(
            [jnp.where(upper, other, vectors), jnp.where(upper, vectors, other)]
        )
        if bit == 1:
            qkv_state = exchange_core(qkv_state)
        if bit == 2:
            qkv_lanes = in_order(qkv_state, pin(out_block))
            for side in range(2):
                enter(side, gather_task("self", side, qkv_lanes[side]))
                visit(side)
                later[side] = waiting[side].pop(0)
    whole_vectors = vectors.transpose(1, 0, 2).reshape(8, width)
    embed, g_attn, b_attn, g_cross, b_cross, g_mlp, b_mlp = [whole_vectors[k] for k in range(7)]

    masked = mask_flags[:, None] == 1
    start = jnp.where(masked, embed[None, :], tokens_in.astype(F32))
    unit_one, inverse_one = normalize(start)
    normed_one = pin((unit_one * g_attn + b_attn).astype(BF16))
    from_x = send(normed_one, swap_x)
    from_core = send(normed_one, swap_core)
    cross_blocks = pin(*cut_columns([cross_key, cross_value, cross_query], head_cut))
    one_near = join_near(normed_one, pin(from_core))
    ring(2)
    from_x = pin(from_x)
    cross_state = exchange_x(cross_blocks)
    one_far = jnp.concatenate([from_x, pin(send(from_x, swap_core))])
    cross_out_block = send(cross_out, to_ranks)
    ring(1)
    cross_state = exchange_core(cross_state)
    ring(1)
    half_text = jnp.stack(
        [
            jnp.where(x == 1, text_states[1], text_states[0]),
            jnp.where(x == 1, text_states[0], text_states[1]),
        ]
    )
    half_text, cross_out_block = pin(half_text, cross_out_block)
    text_x = send(half_text, swap_x)
    text_core = send(half_text, swap_core)
    cross_lanes = in_order(cross_state, cross_out_block)
    for side in range(2):
        enter(side, gather_task("cross", side, cross_lanes[side]))
    in_blocks = pin(*cut_columns([mlp_in], hidden_cut))
    ring(1)
    text_x, text_core = pin(text_x, text_core)
    in_state = exchange_x(in_blocks)
    text_diagonal = pin(send(text_x, swap_core))
    ring(1)
    text_rows = pin(
        jnp.concatenate(
            [
                half_text[0],
                text_x[1],
                text_core[0],
                text_diagonal[1],
                half_text[1],
                text_x[0],
                text_core[1],
                text_diagonal[0],
            ]
        )
    )
    in_state = exchange_core(in_state)
    ring(1)
    back_x = send(out_grad, swap_x)
    back_core = send(out_grad, swap_core)
    in_lanes = in_order(in_state)
    for side in range(2):
        enter(side, gather_task("in", side, in_lanes[side]))
        waiting[side].append(later[side])
    ring(1)

    pair_rows = 2 * rows
    score_flops = 2 * 2 * images * rank_heads * L * DH

    def self_forward(qkv):
        return by_image(
            functools.partial(self_forward_kernel, rank_width, scale),
            [qkv],
            [(L, 3 * rank_width)],
            [(pair_rows, rank_width)],
            [(L, rank_width)],
            2 * score_flops * L,
        )[0]

    def cross_forward(queries, text, skip):
        return by_image(
            functools.partial(cross_forward_kernel, rank_width, scale),
            [queries, text],
            [(L, rank_width), (ctx, 2 * rank_width)],
            [(pair_rows, rank_width)],
            [(L, rank_width)],
            2 * score_flops * ctx,
            skip,
        )[0]

    w_qkv, w_out = settle(
        "self",
        [(block_rows, 3 * rank_width), (own_rows, width)],
        [
            [(block, (0, lane), 0, block, (0, lane))],
            [(block, (0, rank_width), 0, block, (lane, rank_width))] + stacked,
        ],
    )
    qkv_far = pin(product(one_far, w_qkv).astype(BF16))
    mixed_far = self_forward(qkv_far)
    out_far = pin(product(mixed_far, w_out).astype(BF16))
    from_x = send_far(pair(out_far))
    ring(2)
    qkv_near = pin(product(one_near, w_qkv).astype(BF16))
    mixed_near = self_forward(qkv_near)
    out_near = pair(pin(product(mixed_near, w_out)))
    from_core = pin(send(out_near[1].astype(BF16), swap_core))
    back_x, back_core = pin(back_x, back_core)
    back_near = join_near(out_grad, back_core)
    back_far = jnp.concatenate([back_x, send(back_x, swap_core)])
    ring(2)
    first = start + add_near(out_near[0], from_core, pin(from_x))

    unit_two, inverse_two = normalize(first)
    first, normed_two = pin(first, (unit_two * g_cross + b_cross).astype(BF16))
    from_x = send(normed_two, swap_x)
    two_near = join_near(normed_two, pin(send(normed_two, swap_core)))
    ring(2)
    from_x = pin(from_x)
    two_far = jnp.concatenate([from_x, pin(send(from_x, swap_core))])
    ring(2)
    w_text, w_cross_out, w_cross = settle(
        "cross",
        [(block_rows, lane), (own_rows, width), (block_rows, rank_width)],
        [
            [(block, (0, lane), 0, block, (0, lane))],
            [(block, (0, rank_width), 2, block, (0, rank_width))] + stacked,
        ],
    )
    text_kv = pin(product(text_rows, w_text).astype(BF16))
    cross_far = product(two_far, w_cross).astype(BF16)
    cmixed_far = cross_forward(cross_far, text_kv, 2 * images)
    out_far = pin(product(cmixed_far, w_cross_out).astype(BF16))
    from_x = send_far(pair(out_far))
    ring(1)
    cross_near = product(two_near, w_cross).astype(BF16)
    cmixed_near = cross_forward(cross_near, text_kv, 0)
    out_near = pair(pin(product(cmixed_near, w_cross_out)))
    from_core = pin(send(out_near[1].astype(BF16), swap_core))
    ring(1)
    second = first + add_near(out_near[0], from_core, pin(from_x))

    unit_three, inverse_three = normalize(second)
    second, normed_three = pin(second, (unit_three * g_mlp + b_mlp).astype(BF16))
    from_x = send(normed_three, swap_x)
    three_near = join_near(normed_three, pin(send(normed_three, swap_core)))
    ring(2)
    from_x = pin(from_x)
    three_far = jnp.concatenate([from_x, pin(send(from_x, swap_core))])
    three_all = jnp.concatenate([three_near, three_far])
    ring(2)
    ring(2)
    (w_in,) = settle(
        "in",
        [(block_rows, width)],
        [[(block, (0, lane), 0, block, (side * lane, lane))] for side in range(2)],
    )

    def feed(values):
        hidden_pre = product(values, w_in)
        share = 0.5 + 0.5 * lax.erf(hidden_pre * (0.5**0.5))
        bell = jnp.exp(-0.5 * hidden_pre * hidden_pre) * 0.3989422804014327
        return pin((hidden_pre * share).astype(BF16), share + hidden_pre * bell)

    activated_near, slope_near = feed(three_near)
    ring(1)
    activated_far, slope_far = feed(three_far)
    ring(1)
    activated = jnp.concatenate([activated_near, activated_far])
    back_all = jnp.concatenate([back_near, back_far])
    down_part = pin(outer_grad(activated, back_all).astype(BF16)).reshape(n_g, hidden_rows, width)
    ring(2)
    for side in range(2):
        enter(side, reduce_task(("down", side), down_part, side * lane))
    ring(2)

    down_block = (0, hidden_rows)
    (w_down,) = settle(
        "down",
        [(hidden_rows, width)],
        [[(down_block, (0, lane), 0, down_block, (side * lane, lane))] for side in range(2)],
    )
    hidden_far = pin((back_project(back_far, w_down) * slope_far).astype(BF16))
    ring(1)
    three_grad = pin(back_project(hidden_far, w_in).astype(BF16))
    from_x = send_far(pair(three_grad))
    ring(1)
    hidden_near = pin((back_project(back_near, w_down) * slope_near).astype(BF16))
    three_grad = pair(pin(back_project(hidden_near, w_in)))
    from_core = pin(send(three_grad[1].astype(BF16), swap_core))
    ring(2)
    normed_three_grad = add_near(three_grad[0], from_core, pin(from_x))
    rows_three, gain_mlp_term, bias_mlp_term = norm_backward(
        normed_three_grad, unit_three, inverse_three, g_mlp
    )
    second_grad = out_grad.astype(F32) + rows_three
    second_grad, gain_mlp_term, bias_mlp_term, second_low = pin(
        second_grad, gain_mlp_term, bias_mlp_term, second_grad.astype(BF16)
    )
    from_x = send(second_low, swap_x)
    second_near = join_near(second_low, pin(send(second_low, swap_core)))
    hidden_all = jnp.concatenate([hidden_near, hidden_far])
    in_part = pin(outer_grad(three_all, hidden_all).astype(BF16))
    in_part = in_part.reshape(n_g, block_rows, hidden // 4)
    for side in range(2):
        enter(side, reduce_task(("in", side), in_part, side * lane))
    ring(2)

    def by_target(total):
        def rows_of(rel):
            low = (rank[0] ^ rel) * own_rows
            return lax.dynamic_slice(total, (low, 0), (own_rows, total.shape[1])).astype(BF16)

        return (rows_of(0), jnp.stack([rows_of(1), rows_of(3)]), rows_of(2))

    def stack_rows(part):
        cut = part.reshape(n_g, own_rows, width)
        size = width // 4
        return jnp.concatenate([cut[:, :, k * size : (k + 1) * size] for k in range(4)], axis=1)

    def unstack_rows(total):
        return jnp.concatenate(
            [total[k * own_rows : (k + 1) * own_rows] for k in range(4)], axis=1
        ).astype(BF16)

    def cross_backward(queries, text, grads, skip):
        return by_image(
            functools.partial(cross_backward_kernel, rank_width, scale),
            [queries, text, grads],
            [(L, rank_width), (ctx, 2 * rank_width), (L, rank_width)],
            [(pair_rows, rank_width), (2 * images * ctx, 2 * rank_width)],
            [(L, rank_width), (ctx, 2 * rank_width)],
            5 * score_flops * ctx,
            skip,
        )

    from_x = pin(from_x)
    second_far = jnp.concatenate([from_x, pin(send(from_x, swap_core))])
    cgrad_far = back_project(second_far, w_cross_out).astype(BF16)
    cq_far, tkv_far = cross_backward(cross_far, text_kv, cgrad_far, 2 * images)
    two_grad = pin(back_project(cq_far, w_cross).astype(BF16))
    from_x = send_far(pair(two_grad))
    ring(2)
    cgrad_near = back_project(second_near, w_cross_out).astype(BF16)
    cq_near, tkv_near = cross_backward(cross_near, text_kv, cgrad_near, 0)
    two_grad = pair(pin(back_project(cq_near, w_cross)))
    from_core = pin(send(two_grad[1].astype(BF16), swap_core))
    cmixed_all = jnp.concatenate([cmixed_near, cmixed_far])
    second_all = jnp.concatenate([second_near, second_far])
    cross_out_part = pin(outer_grad(cmixed_all, second_all).astype(BF16))
    ring(2)
    normed_two_grad = add_near(two_grad[0], from_core, pin(from_x))
    rows_two, gain_cross_term, bias_cross_term = norm_backward(
        normed_two_grad, unit_two, inverse_two, g_cross
    )
    first_grad = second_grad + rows_two
    first_grad, gain_cross_term, bias_cross_term, first_low = pin(
        first_grad, gain_cross_term, bias_cross_term, first_grad.astype(BF16)
    )
    from_x = send(first_low, swap_x)
    first_near = join_near(first_low, pin(send(first_low, swap_core)))
    two_all = jnp.concatenate([two_near, two_far])
    cq_all = jnp.concatenate([cq_near, cq_far])
    tkv_all = jnp.concatenate([tkv_near, tkv_far])
    cross_part = pin(outer_grad(two_all, cq_all).astype(BF16))
    ring(1)
    text_kv_part = pin(outer_grad(text_rows, tkv_all).astype(BF16))
    text_kv_part = text_kv_part.reshape(n_g, block_rows, lane)
    cross_part = cross_part.reshape(n_g, block_rows, rank_width)
    cross_part = jnp.concatenate([cross_part, stack_rows(cross_out_part)], axis=2)
    enter(0, reduce_task(("cross", 0), text_kv_part, 0))
    enter(1, reduce_task(("cross", 1), cross_part, 0))
    ring(1)
    sgrad_near = pin(back_project(first_near, w_out).astype(BF16))

    def self_backward(qkv, grads):
        return by_image(
            functools.partial(self_backward_kernel, rank_width, scale),
            [qkv, grads],
            [(L, 3 * rank_width), (L, rank_width)],
            [(pair_rows, 3 * rank_width)],
            [(L, 3 * rank_width)],
            5 * score_flops * L,
        )[0]

    qkv_grad_near = pin(self_backward(qkv_near, sgrad_near))
    from_x = pin(from_x)
    first_far = jnp.concatenate([from_x, pin(send(from_x, swap_core))])
    ring(2)
    sgrad_far = back_project(first_far, w_out).astype(BF16)
    qkv_grad_far = self_backward(qkv_far, sgrad_far)
    one_grad = pin(back_project(qkv_grad_far, w_qkv).astype(BF16))
    from_x = send_far(pair(one_grad))
    ring(1)
    one_all = jnp.concatenate([one_near, one_far])
    qkv_grad_all = jnp.concatenate([qkv_grad_near, qkv_grad_far])
    qkv_part = pin(outer_grad(one_all, qkv_grad_all).astype(BF16))
    ring(1)
    mixed_all = jnp.concatenate([mixed_near, mixed_far])
    first_all = jnp.concatenate([first_near, first_far])
    out_part = pin(outer_grad(mixed_all, first_all).astype(BF16))
    qkv_part = qkv_part.reshape(n_g, block_rows, 3 * rank_width)
    enter(0, reduce_task(("self", 0), qkv_part, 0))
    last_part = jnp.concatenate([qkv_part[:, :, lane:], stack_rows(out_part)], axis=2)
    enter(1, reduce_task(("self", 1), last_part, 0))
    ring(1)
    one_grad = pair(pin(back_project(qkv_grad_near, w_qkv)))
    from_core = pin(send(one_grad[1].astype(BF16), swap_core))
    ring(1)
    normed_one_grad = add_near(one_grad[0], from_core, pin(from_x))
    rows_one, gain_attn_term, bias_attn_term = norm_backward(
        normed_one_grad, unit_one, inverse_one, g_attn
    )
    start_grad = first_grad + rows_one
    tokens_grad = jnp.where(masked, 0.0, start_grad)
    embed_term = jnp.sum(jnp.where(masked, start_grad, 0.0), axis=0)
    tokens_grad, embed_term, gain_attn_term, bias_attn_term = pin(
        tokens_grad, embed_term, gain_attn_term, bias_attn_term
    )

    result_far = pin(product(activated_far, w_down).astype(BF16))
    ring(1)
    from_x = send_far(pair(result_far))
    result_near = pair(pin(product(activated_near, w_down)))
    from_core = pin(send(result_near[1].astype(BF16), swap_core))
    ring(2)
    text_part = pin(back_project(tkv_all, w_text)).reshape(8, ctx // 2, width)
    output = pin((second + add_near(result_near[0], from_core, pin(from_x))).astype(BF16))
    text_own = jnp.stack([text_part[0], text_part[4]])
    text_far = [
        jnp.stack([text_part[a], text_part[b]]).astype(BF16) for a, b in ((5, 1), (2, 6), (7, 3))
    ]
    from_x = send_far([text_far[0], text_far[2]])
    from_core = pin(send(text_far[1], swap_core))
    ring(2)
    text_sum = add_near(text_own, from_core, pin(from_x))
    text_grad = pin(
        jnp.stack(
            [
                jnp.where(x == 1, text_sum[1], text_sum[0]),
                jnp.where(x == 1, text_sum[0], text_sum[1]),
            ]
        )
    )
    in_sum = jnp.concatenate([summed(("in", 0)), summed(("in", 1))], axis=1)
    in_state = exchange_core(exchange_x(by_target(in_sum)))
    ring(2)
    (mlp_in_grad,) = join_columns(*exchange_end(in_state), hidden_cut, 1)
    mlp_in_grad = pin(mlp_in_grad)
    mlp_out_grad = pin(jnp.concatenate([summed(("down", 0)), summed(("down", 1))], axis=1))

    terms = jnp.stack(
        [
            embed_term,
            gain_attn_term,
            bias_attn_term,
            gain_cross_term,
            bias_cross_term,
            gain_mlp_term,
            bias_mlp_term,
            jnp.zeros_like(bias_mlp_term),
        ]
    )
    terms = terms.reshape(8, n, own_rows).transpose(1, 0, 2)
    for bit in reversed(range(bits)):
        upper = (me >> bit) & 1 == 1
        count = terms.shape[0] // 2
        keep = jnp.where(upper, terms[count:], terms[:count])
        away = jnp.where(upper, terms[:count], terms[count:])
        terms = keep + pin(send(away, [(i, i ^ (1 << bit)) for i in range(n)]))
    terms = terms[0]

    text_kv_sum = summed(("cross", 0))
    cross_sum = summed(("cross", 1))
    cross_total = jnp.concatenate([text_kv_sum, cross_sum[:, :rank_width]], axis=1)
    cross_state = exchange_x(by_target(cross_total))
    cross_out_grad = send(unstack_rows(cross_sum[:, rank_width:]), from_ranks)
    ring(1)
    cross_state = exchange_core(cross_state)
    ring(1)
    cross_key_grad, cross_value_grad, cross_query_grad = join_columns(
        *exchange_end(cross_state), head_cut, 3
    )
    cross_query_grad, cross_key_grad, cross_value_grad, cross_out_grad = pin(
        cross_query_grad, cross_key_grad, cross_value_grad, cross_out_grad.astype(F32)
    )
    qkv_sum = summed(("self", 0))
    last_sum = summed(("self", 1))
    qkv_sum = jnp.concatenate([qkv_sum, last_sum[:, :rank_width]], axis=1)
    attn_out_grad = send(unstack_rows(last_sum[:, rank_width:]), from_ranks).astype(F32)
    qkv_state = exchange_core(exchange_x(by_target(qkv_sum)))
    attn_query_grad, attn_key_grad, attn_value_grad = join_columns(
        *exchange_end(qkv_state), head_cut, 3
    )

    return (
        output,
        tokens_grad,
        text_grad,
        terms[0],
        terms[1],
        terms[2],
        attn_query_grad,
        attn_key_grad,
        attn_value_grad,
        attn_out_grad,
        terms[3],
        terms[4],
        cross_query_grad,
        cross_key_grad,
        cross_value_grad,
        cross_out_grad,
        terms[5],
        terms[6],
        mlp_in_grad,
        mlp_out_grad,
    )


def solution(mesh):
    devices = mesh.devices.reshape(mesh.shape["dp"] // 2, 2, mesh.shape["text"])
    groups = jax.sharding.Mesh(devices, ("g", "core", "x"))
    spec_rows = P(AXES, None)
    spec_text = P(("g", "core"), "x", None)
    spec_vector = P(AXES)
    return jax.shard_map(
        functools.partial(on_device, groups.shape["g"]),
        mesh=groups,
        in_specs=(spec_rows, spec_vector, spec_text)
        + (spec_vector,) * 3
        + (spec_rows,) * 4
        + (spec_vector,) * 2
        + (spec_rows,) * 4
        + (spec_vector,) * 2
        + (spec_rows,) * 3,
        out_specs=(spec_rows, spec_rows, spec_text)
        + (spec_vector,) * 3
        + (spec_rows,) * 4
        + (spec_vector,) * 2
        + (spec_rows,) * 4
        + (spec_vector,) * 2
        + (spec_rows,) * 2,
        check_vma=False,
    )
```

```python
import functools

import jax
import jax.numpy as jnp
from jax import lax
from jax.experimental import pallas as pl
from jax.experimental.pallas import tpu as pltpu
from jax.sharding import PartitionSpec as P

DH = 128
L = 256
AXES = ("g", "core", "x")
F32 = jnp.float32
BF16 = jnp.bfloat16
epsilon = 1e-06


def normalize(rows):
    mean = jnp.mean(rows, axis=-1, keepdims=True)
    centered = rows - mean
    inverse = lax.rsqrt(jnp.mean(centered * centered, axis=-1, keepdims=True) + epsilon)
    return (centered * inverse, inverse)


def norm_backward(grad_out, unit_rows, inverse, gain):
    scaled = grad_out * gain
    mean_grad = jnp.mean(scaled, axis=-1, keepdims=True)
    mean_mixed = jnp.mean(scaled * unit_rows, axis=-1, keepdims=True)
    rows_grad = inverse * (scaled - mean_grad - unit_rows * mean_mixed)
    return (rows_grad, jnp.sum(grad_out * unit_rows, axis=0), jnp.sum(grad_out, axis=0))


def product(left, right):
    return jnp.dot(left, right, preferred_element_type=F32)


def outer_grad(left, right):
    return lax.dot_general(left, right, (((0,), (0,)), ((), ())), preferred_element_type=F32)


def back_project(left, right):
    return lax.dot_general(left, right, (((1,), (1,)), ((), ())), preferred_element_type=F32)


def forward_head(query, key, value, scale):
    scores = back_project(query, key) * scale
    exps = jnp.exp(scores - jnp.max(scores, axis=1, keepdims=True))
    weights = exps * (1.0 / jnp.sum(exps, axis=1, keepdims=True))
    return product(weights.astype(BF16), value).astype(BF16)


def backward_head(query, key, value, mixed_grad, scale):
    scores = back_project(key, query) * scale
    exps = jnp.exp(scores - jnp.max(scores, axis=0, keepdims=True))
    weights = exps * (1.0 / jnp.sum(exps, axis=0, keepdims=True))
    value_grad = product(weights.astype(BF16), mixed_grad)
    weight_grad = back_project(value, mixed_grad)
    delta = jnp.sum(weights * weight_grad, axis=0, keepdims=True)
    score_grad = (weights * (weight_grad - delta)).astype(BF16)
    query_grad = outer_grad(score_grad, key) * scale
    key_grad = product(score_grad, query) * scale
    return (query_grad.astype(BF16), key_grad.astype(BF16), value_grad.astype(BF16))


def self_forward_kernel(width, scale, qkv, mixed):
    for low in range(0, width, DH):
        at = [slice(part * width + low, part * width + low + DH) for part in range(3)]
        mixed[:, at[0]] = forward_head(qkv[:, at[0]], qkv[:, at[1]], qkv[:, at[2]], scale)


def self_backward_kernel(width, scale, qkv, mixed_grad, grads):
    for low in range(0, width, DH):
        at = [slice(part * width + low, part * width + low + DH) for part in range(3)]
        terms = backward_head(
            qkv[:, at[0]], qkv[:, at[1]], qkv[:, at[2]], mixed_grad[:, at[0]], scale
        )
        for part in range(3):
            grads[:, at[part]] = terms[part]


def cross_forward_kernel(width, scale, queries, text, mixed):
    for low in range(0, width, DH):
        at = [slice(part * width + low, part * width + low + DH) for part in range(2)]
        mixed[:, at[0]] = forward_head(queries[:, at[0]], text[:, at[0]], text[:, at[1]], scale)


def cross_backward_kernel(width, scale, queries, text, mixed_grad, query_grads, text_grads):
    for low in range(0, width, DH):
        at = [slice(part * width + low, part * width + low + DH) for part in range(2)]
        terms = backward_head(
            queries[:, at[0]], text[:, at[0]], text[:, at[1]], mixed_grad[:, at[0]], scale
        )
        query_grads[:, at[0]] = terms[0]
        text_grads[:, at[0]] = terms[1]
        text_grads[:, at[1]] = terms[2]


def by_image(kernel, args, blocks, shapes, out_blocks, flops, skip=0):
    images = shapes[0][0] // out_blocks[0][0]
    offsets = [0 if arg.shape[0] // block[0] == images else skip for arg, block in zip(args, blocks)]
    total = sum(images * block[0] * block[1] * 2 for block in (*blocks, *out_blocks))
    return pl.pallas_call(
        kernel,
        grid=(images,),
        in_specs=[
            pl.BlockSpec(block, functools.partial(lambda off, i: (i + off, 0), off))
            for block, off in zip(blocks, offsets)
        ],
        out_specs=[pl.BlockSpec(block, lambda i: (i, 0)) for block in out_blocks],
        out_shape=[jax.ShapeDtypeStruct(shape, BF16) for shape in shapes],
        compiler_params=pltpu.CompilerParams(vmem_limit_bytes=32 * 1024 * 1024),
        cost_estimate=pl.CostEstimate(
            flops=flops, bytes_accessed=total, transcendentals=flops // 512
        ),
    )(*args)


def head_start(piece, rank):
    return DH * (4 * piece + 2 * (rank & 1) + (rank >> 1))


def hidden_start(size, piece, rank):
    return size * (4 * piece + rank)


def lanes_at(start, size):
    return pl.ds(pl.multiple_of(start, 128), size)


def cut_kernel(start, pieces, size, rank_ref, *refs):
    weights, (own, to_x, to_core) = refs[:-3], refs[-3:]
    for rel, out in ((0, own), (1, to_x.at[0]), (3, to_x.at[1]), (2, to_core)):
        rank = rank_ref[0] ^ rel
        for k, weight in enumerate(weights):
            for piece in range(pieces):
                column = (k * pieces + piece) * size
                out[:, column : column + size] = weight[:, lanes_at(start(piece, rank), size)]


def join_kernel(start, pieces, size, rank_ref, own, from_x, from_core, *outs):
    for rel, source in ((0, own), (1, from_x.at[0]), (2, from_core.at[0]), (3, from_core.at[1])):
        rank = rank_ref[0] ^ rel
        for k, out in enumerate(outs):
            for piece in range(pieces):
                column = (k * pieces + piece) * size
                value = source[:, column : column + size].astype(F32)
                out[:, lanes_at(start(piece, rank), size)] = value


def order_kernel(rank_ref, own, from_x, from_core, *refs):
    extra, out = refs[:-1], refs[-1]
    rows, columns = own.shape
    for rel, source in ((0, own), (1, from_x.at[0]), (2, from_core.at[0]), (3, from_core.at[1])):
        at = pl.ds(pl.multiple_of((rank_ref[0] ^ rel) * rows, rows), rows)
        out[at, :columns] = source[...]
    for weight in extra:
        size = weight.shape[1] // 4
        for part in range(4):
            piece = weight[:, part * size : (part + 1) * size]
            out[part * rows : (part + 1) * rows, columns:] = piece


def assemble_kernel(plan, count, places_ref, *refs):
    sources, refs = refs[:count], refs[count:]
    outs, held, loaded, stored = refs[: -2 - count], refs[-2 - count : -2], refs[-2], refs[-1]
    loads = [
        pltpu.make_async_copy(source, buffer, loaded.at[k])
        for k, (source, buffer) in enumerate(zip(sources, held))
    ]
    for load in loads:
        load.start()
    stores = []
    for load, buffer, (place, moves) in zip(loads, held, plan):
        load.wait()
        for rows, columns, out, to_rows, to_columns in moves:
            stores.append(
                pltpu.make_async_copy(
                    buffer.at[pl.ds(*rows), pl.ds(*columns)],
                    outs[out].at[places_ref[place], pl.ds(*to_rows), pl.ds(*to_columns)],
                    stored.at[len(stores)],
                )
            )
            stores[-1].start()
    for store in stores:
        store.wait()


def whole_call(kernel, rank, args, shapes, dtype):
    moved = 2 * sum(arg.size * arg.dtype.itemsize for arg in args)
    return pl.pallas_call(
        kernel,
        in_specs=[pl.BlockSpec(memory_space=pltpu.SMEM)]
        + [pl.BlockSpec(memory_space=pltpu.VMEM)] * len(args),
        out_specs=[pl.BlockSpec(memory_space=pltpu.VMEM)] * len(shapes),
        out_shape=[jax.ShapeDtypeStruct(shape, dtype) for shape in shapes],
        compiler_params=pltpu.CompilerParams(vmem_limit_bytes=24 * 1024 * 1024),
        cost_estimate=pl.CostEstimate(flops=0, bytes_accessed=moved, transcendentals=0),
    )(rank, *args)


def assemble(plan, places, pieces, shapes):
    count = sum(len(moves) for place, moves in plan)
    return pl.pallas_call(
        functools.partial(assemble_kernel, plan, len(pieces)),
        in_specs=[pl.BlockSpec(memory_space=pltpu.SMEM)]
        + [pl.BlockSpec(memory_space=pl.ANY)] * len(pieces),
        out_specs=[pl.BlockSpec(memory_space=pl.ANY)] * len(shapes),
        out_shape=[jax.ShapeDtypeStruct(shape, BF16) for shape in shapes],
        scratch_shapes=[pltpu.VMEM(piece.shape, BF16) for piece in pieces]
        + [pltpu.SemaphoreType.DMA((len(pieces),)), pltpu.SemaphoreType.DMA((count,))],
        compiler_params=pltpu.CompilerParams(vmem_limit_bytes=40 * 1024 * 1024),
        cost_estimate=pl.CostEstimate(flops=0, bytes_accessed=1 << 20, transcendentals=0),
    )(places, *pieces)


def on_device(
    n_g,
    tokens_in,
    mask_flags,
    text_states,
    mask_embed,
    gain_attn,
    bias_attn,
    attn_query,
    attn_key,
    attn_value,
    attn_out,
    gain_cross,
    bias_cross,
    cross_query,
    cross_key,
    cross_value,
    cross_out,
    gain_mlp,
    bias_mlp,
    mlp_in,
    mlp_out,
    out_grad,
):
    n = n_g * 4
    half_ring = n_g // 2
    rows, width = tokens_in.shape
    own_rows = attn_query.shape[0]
    hidden = mlp_in.shape[1]
    heads = width // DH
    rank_heads = heads // 4
    rank_width = rank_heads * DH
    parts = n // heads
    ctx = 2 * text_states.shape[1]
    images = rows // L
    scale = DH ** (-0.5)

    g = lax.axis_index("g")
    core = lax.axis_index("core")
    x = lax.axis_index("x")

    order = list(range(0, n_g, 2)) + list(range(n_g - 1, 0, -2))
    ahead = {order[p]: order[(p + 1) % n_g] for p in range(n_g)}
    swap_x = [(i, i ^ 1) for i in range(n)]
    swap_core = [(i, i ^ 2) for i in range(n)]
    go_next = [(i, ahead[i // 4] * 4 + i % 4) for i in range(n)]
    go_prev = [(j, i) for i, j in go_next]
    place = jnp.where((g & 1) == 0, g >> 1, n_g - 1 - (g >> 1))

    def g_at(offset):
        p = place + (offset % n_g)
        p = jnp.where(p >= n_g, p - n_g, p)
        return jnp.where(p < half_ring, 2 * p, 2 * (n_g - 1 - p) + 1)

    def send(value, pairs):
        return lax.ppermute(value, AXES, pairs)

    token = mask_flags

    def pin(*values):
        nonlocal token
        values, token = lax.optimization_barrier((values, token))
        return values if len(values) > 1 else values[0]

    def flip(blocks):
        blocks = [jnp.where(x == 1, blocks[k ^ 1], blocks[k]) for k in range(4)]
        return [jnp.where(core == 1, blocks[k ^ 2], blocks[k]) for k in range(4)]

    me = g * 4 + core * 2 + x
    rank = jnp.reshape(core * 2 + x, (1,)).astype(jnp.int32)
    hidden_rows = mlp_out.shape[0]
    head_cut = (head_start, rank_heads, DH)
    hidden_cut = (functools.partial(hidden_start, hidden_rows), n_g, hidden_rows)

    def pieces_of(cut, size):
        return [[int(cut[0](piece, to)) for piece in range(cut[1])] for to in range(4)]

    def cut_columns(weights, cut):
        start, pieces, size = cut
        if size % 128 == 0:
            shape = (own_rows, len(weights) * pieces * size)
            kernel = functools.partial(cut_kernel, start, pieces, size)
            return whole_call(kernel, pin(rank), weights, [shape, (2,) + shape, shape], BF16)
        rel = flip(
            [
                jnp.concatenate(
                    [weight[:, low : low + size] for weight in weights for low in lows], axis=1
                )
                for lows in pieces_of(cut, size)
            ]
        )
        return (rel[0], jnp.stack([rel[1], rel[3]]), rel[2])

    def join_columns(own, from_x, from_core, cut, count):
        start, pieces, size = cut
        if size % 128 == 0:
            shape = (own_rows, 4 * pieces * size)
            kernel = functools.partial(join_kernel, start, pieces, size)
            return whole_call(kernel, rank, [own, from_x, from_core], [shape] * count, F32)
        blocks = flip([own, from_x[0], from_core[0], from_core[1]])
        outs = []
        for k in range(count):
            found = sorted(
                (low, to, k * pieces + piece)
                for to, lows in enumerate(pieces_of(cut, size))
                for piece, low in enumerate(lows)
            )
            parts = [blocks[to][:, at * size : (at + 1) * size] for low, to, at in found]
            outs.append(jnp.concatenate(parts, axis=1).astype(F32))
        return outs

    def exchange_x(blocks):
        own, to_x, to_core = blocks
        return (own, to_core, send(to_x, swap_x))

    def exchange_core(state):
        own, to_core, from_x = state
        from_x = pin(from_x)
        return (own, from_x, send(jnp.stack([to_core, from_x[1]]), swap_core))

    def exchange_end(state):
        own, from_x, from_core = state
        return (own, from_x, pin(from_core))

    def in_order(state, *extra):
        values = list(exchange_end(state)) + list(extra)
        return whole_call(order_kernel, rank, values, [(4 * own_rows, width)], BF16)[0]

    pieces = {}
    under_way = {"self", "cross", "in", "down"}
    sums = {}
    places = jnp.stack([g_at(offset) for offset in range(n_g)]).astype(jnp.int32)

    def gather_task(name, block):
        found = pieces.setdefault(name, [(block, 0, 0)])
        clock = counter = block
        half = block.shape[0] // 2
        for step in range(1, half_ring + 1):
            if step == half_ring:
                clock, counter = clock[:half], counter[half:]
            clock, counter = yield [(clock, go_next), (counter, go_prev)]
            found.append((clock, -step % n_g, 0))
            found.append((counter, step, half if step == half_ring else 0))
        under_way.remove(name)

    def reduce_task(name, *parts):
        def mine(offset):
            where = g_at(offset)
            blocks = []
            for part in parts:
                block = lax.dynamic_index_in_dim(part, where, 0, keepdims=False)
                if block.shape[0] != parts[0].shape[1]:
                    block = jnp.concatenate(jnp.split(block, 4, axis=1))
                blocks.append(block)
            return jnp.concatenate(blocks, axis=1) if len(blocks) > 1 else blocks[0]

        block = mine(half_ring)
        half = block.shape[0] // 2
        clock, counter = block[:half], block[half:]
        for step in range(half_ring - 1, -1, -1):
            clock, counter = yield [(clock, go_next), (counter, go_prev)]
            clock, counter = clock.astype(F32), counter.astype(F32)
            up, down = mine(step).astype(F32), mine(-step).astype(F32)
            if step == half_ring - 1:
                clock = jnp.concatenate([up[:half] + clock, up[half:]]).astype(BF16)
                counter = jnp.concatenate([down[:half], down[half:] + counter]).astype(BF16)
            elif step:
                clock, counter = (up + clock).astype(BF16), (down + counter).astype(BF16)
        sums[name] = up + clock + counter

    waiting = []
    flying = []

    def launch():
        if waiting and not flying:
            task, sends = waiting.pop(0)
            if sends is None:
                sends = next(task)
            else:
                values = pin(*[value for value, pairs in sends])
                sends = [(value, pairs) for value, (old, pairs) in zip(values, sends)]
            flying.append((task, [send(*item) for item in sends]))

    def enter(task):
        waiting.append((task, None))
        launch()

    def ring(hold=False):
        held = None
        if flying:
            task, flight = flying.pop()
            try:
                sends = task.send(pin(*flight))
                if hold:
                    held = (task, sends)
                else:
                    flying.append((task, [send(*item) for item in sends]))
            except StopIteration:
                pass
            launch()
        return held

    def ring_with(*values):
        task, flight = flying.pop()
        got = pin(*flight, *values)
        flying.append((task, list(got[: len(flight)])))
        ring()
        return got[len(flight) :]

    def settle(name, shapes, moves):
        while name in under_way:
            ring()
        plan = []
        for value, place, low in pieces[name]:
            high = low + value.shape[0]
            inside = []
            for (row, size), columns, out, (to_row, unused), to_columns in moves:
                first, last = max(row, low), min(row + size, high)
                if first < last:
                    to = (to_row + first - row, last - first)
                    inside.append(((first - low, last - first), columns, out, to, to_columns))
            plan.append((place, inside))
        values = [value for value, place, low in pieces[name]]
        shapes = [(n_g,) + shape for shape in shapes]
        outs = assemble(plan, places, values, shapes)
        return [out.reshape(n_g * out.shape[1], out.shape[2]) for out in outs]

    def summed(name):
        while name not in sums:
            ring()
        return sums[name]

    def join_near(value, from_core):
        return jnp.concatenate([value, from_core])

    def send_far(far):
        from_diagonal = pin(send(far[1], swap_core))
        across = pin((far[0].astype(F32) + from_diagonal.astype(F32)).astype(BF16))
        return send(across, swap_x)

    def add_near(near, from_core, from_x):
        return near + from_x.astype(F32) + from_core.astype(F32)

    def pair(value):
        return value.reshape((2, value.shape[0] // 2) + value.shape[1:])

    to_ranks = []
    for i in range(n):
        head, part = i // parts, i % parts
        to_ranks.append((i, ((head // 4) * parts + part) * 4 + (head % 2) * 2 + (head // 2) % 2))
    from_ranks = [(j, i) for i, j in to_ranks]

    block_rows = 4 * own_rows
    block = (0, block_rows)
    stacked = [
        ((part * own_rows, own_rows), (3 * rank_width, rank_width), 1, (0, own_rows), (part * rank_width, rank_width))
        for part in range(4)
    ]

    enter(gather_task("down", mlp_out))
    qkv_state = exchange_x(cut_columns([attn_query, attn_key, attn_value], head_cut))
    vectors = jnp.stack(
        [
            mask_embed,
            gain_attn,
            bias_attn,
            gain_cross,
            bias_cross,
            gain_mlp,
            bias_mlp,
            jnp.zeros_like(bias_mlp),
        ]
    ).astype(F32)[None]

    bits = n.bit_length() - 1
    out_block = send(attn_out, to_ranks)
    for bit in range(bits):
        other = pin(send(vectors, [(i, i ^ (1 << bit)) for i in range(n)]))
        upper = (me >> bit) & 1 == 1
        vectors = jnp.concatenate(
            [jnp.where(upper, other, vectors), jnp.where(upper, vectors, other)]
        )
        if bit == 1:
            qkv_state = exchange_core(qkv_state)
        if bit == 2:
            enter(gather_task("self", in_order(qkv_state, pin(out_block))))
            later = ring(hold=True)
    whole_vectors = vectors.transpose(1, 0, 2).reshape(8, width)
    embed, g_attn, b_attn, g_cross, b_cross, g_mlp, b_mlp = [whole_vectors[k] for k in range(7)]

    masked = mask_flags[:, None] == 1
    start = jnp.where(masked, embed[None, :], tokens_in.astype(F32))
    unit_one, inverse_one = normalize(start)
    normed_one = pin((unit_one * g_attn + b_attn).astype(BF16))
    from_x = send(normed_one, swap_x)
    from_core = send(normed_one, swap_core)
    cross_blocks = pin(*cut_columns([cross_key, cross_value, cross_query], head_cut))
    one_near = join_near(normed_one, pin(from_core))
    ring()
    from_x = pin(from_x)
    cross_state = exchange_x(cross_blocks)
    cross_out_block = send(cross_out, to_ranks)
    one_far = jnp.concatenate([from_x, pin(send(from_x, swap_core))])
    cross_state = exchange_core(cross_state)
    ring()
    half_text = jnp.stack(
        [
            jnp.where(x == 1, text_states[1], text_states[0]),
            jnp.where(x == 1, text_states[0], text_states[1]),
        ]
    )
    half_text, cross_out_block = pin(half_text, cross_out_block)
    text_x = send(half_text, swap_x)
    text_core = send(half_text, swap_core)
    enter(gather_task("cross", in_order(cross_state, cross_out_block)))
    in_blocks = pin(*cut_columns([mlp_in], hidden_cut))
    text_x, text_core = pin(text_x, text_core)
    in_state = exchange_x(in_blocks)
    text_diagonal = pin(send(text_x, swap_core))
    ring()
    in_state = exchange_core(in_state)
    back_x = send(out_grad, swap_x)
    back_core = send(out_grad, swap_core)
    text_rows = pin(
        jnp.concatenate(
            [
                half_text[0],
                text_x[1],
                text_core[0],
                text_diagonal[1],
                half_text[1],
                text_x[0],
                text_core[1],
                text_diagonal[0],
            ]
        )
    )
    enter(gather_task("in", in_order(in_state)))
    ring()
    waiting.append(later)

    pair_rows = 2 * rows
    score_flops = 2 * 2 * images * rank_heads * L * DH

    def self_forward(qkv):
        return by_image(
            functools.partial(self_forward_kernel, rank_width, scale),
            [qkv],
            [(L, 3 * rank_width)],
            [(pair_rows, rank_width)],
            [(L, rank_width)],
            2 * score_flops * L,
        )[0]

    def cross_forward(queries, text, skip):
        return by_image(
            functools.partial(cross_forward_kernel, rank_width, scale),
            [queries, text],
            [(L, rank_width), (ctx, 2 * rank_width)],
            [(pair_rows, rank_width)],
            [(L, rank_width)],
            2 * score_flops * ctx,
            skip,
        )[0]

    w_qkv, w_out = settle(
        "self",
        [(block_rows, 3 * rank_width), (own_rows, width)],
        [(block, (0, 3 * rank_width), 0, block, (0, 3 * rank_width))] + stacked,
    )
    back_x, back_core = pin(back_x, back_core)
    qkv_far = pin(product(one_far, w_qkv).astype(BF16))
    ring()
    mixed_far = self_forward(qkv_far)
    out_far = pin(product(mixed_far, w_out).astype(BF16))
    from_x = send_far(pair(out_far))
    qkv_near = pin(product(one_near, w_qkv).astype(BF16))
    mixed_near = self_forward(qkv_near)
    out_near = pair(pin(product(mixed_near, w_out)))
    from_core = pin(send(out_near[1].astype(BF16), swap_core))
    ring()
    back_near = join_near(out_grad, back_core)
    back_far = jnp.concatenate([back_x, send(back_x, swap_core)])
    first = start + add_near(out_near[0], from_core, pin(from_x))

    unit_two, inverse_two = normalize(first)
    first, normed_two = pin(first, (unit_two * g_cross + b_cross).astype(BF16))
    from_x = send(normed_two, swap_x)
    two_near = join_near(normed_two, pin(send(normed_two, swap_core)))
    ring()
    from_x = pin(from_x)
    two_far = jnp.concatenate([from_x, pin(send(from_x, swap_core))])
    ring()
    w_text, w_cross_out, w_cross = settle(
        "cross",
        [(block_rows, 2 * rank_width), (own_rows, width), (block_rows, rank_width)],
        [
            (block, (0, 2 * rank_width), 0, block, (0, 2 * rank_width)),
            (block, (2 * rank_width, rank_width), 2, block, (0, rank_width)),
        ]
        + stacked,
    )
    text_kv = pin(product(text_rows, w_text).astype(BF16))
    ring()
    cross_far = product(two_far, w_cross).astype(BF16)
    cmixed_far = cross_forward(cross_far, text_kv, 2 * images)
    out_far = pin(product(cmixed_far, w_cross_out).astype(BF16))
    from_x = send_far(pair(out_far))
    cross_near = product(two_near, w_cross).astype(BF16)
    cmixed_near = cross_forward(cross_near, text_kv, 0)
    out_near = pair(pin(product(cmixed_near, w_cross_out)))
    from_core = pin(send(out_near[1].astype(BF16), swap_core))
    ring()
    second = first + add_near(out_near[0], from_core, pin(from_x))

    unit_three, inverse_three = normalize(second)
    second, normed_three = pin(second, (unit_three * g_mlp + b_mlp).astype(BF16))
    from_x = send(normed_three, swap_x)
    three_near = join_near(normed_three, pin(send(normed_three, swap_core)))
    ring()
    from_x = pin(from_x)
    three_far = jnp.concatenate([from_x, pin(send(from_x, swap_core))])
    three_all = jnp.concatenate([three_near, three_far])
    ring()
    (w_in,) = settle(
        "in", [(block_rows, width)], [(block, (0, width), 0, block, (0, width))]
    )

    def feed(values):
        hidden_pre = product(values, w_in)
        share = 0.5 + 0.5 * lax.erf(hidden_pre * (0.5**0.5))
        bell = jnp.exp(-0.5 * hidden_pre * hidden_pre) * 0.3989422804014327
        return pin((hidden_pre * share).astype(BF16), share + hidden_pre * bell)

    activated_near, slope_near = feed(three_near)
    ring()
    activated_far, slope_far = feed(three_far)
    ring()
    activated = jnp.concatenate([activated_near, activated_far])
    back_all = jnp.concatenate([back_near, back_far])
    down_part = pin(outer_grad(activated, back_all).astype(BF16)).reshape(n_g, hidden_rows, width)
    enter(reduce_task("down", down_part))
    ring()

    down_block = (0, hidden_rows)
    (w_down,) = settle(
        "down", [(hidden_rows, width)], [(down_block, (0, width), 0, down_block, (0, width))]
    )
    w_down = pin(w_down)
    ring()
    hidden_far = pin((back_project(back_far, w_down) * slope_far).astype(BF16))
    ring()
    three_grad = pin(back_project(hidden_far, w_in).astype(BF16))
    from_x = send_far(pair(three_grad))
    hidden_near = pin((back_project(back_near, w_down) * slope_near).astype(BF16))
    (from_x,) = ring_with(from_x)
    hidden_all = jnp.concatenate([hidden_near, hidden_far])
    in_part = pin(outer_grad(three_all, hidden_all).astype(BF16))
    in_part = in_part.reshape(n_g, block_rows, hidden // 4)
    enter(reduce_task("in", in_part))
    ring()
    three_grad = pair(pin(back_project(hidden_near, w_in)))
    from_core = pin(send(three_grad[1].astype(BF16), swap_core))
    normed_three_grad = add_near(three_grad[0], from_core, from_x)
    rows_three, gain_mlp_term, bias_mlp_term = norm_backward(
        normed_three_grad, unit_three, inverse_three, g_mlp
    )
    second_grad = out_grad.astype(F32) + rows_three
    second_grad, gain_mlp_term, bias_mlp_term, second_low = pin(
        second_grad, gain_mlp_term, bias_mlp_term, second_grad.astype(BF16)
    )
    from_x = send(second_low, swap_x)
    second_near = join_near(second_low, pin(send(second_low, swap_core)))
    ring()

    def by_target(total):
        def rows_of(rel):
            low = (rank[0] ^ rel) * own_rows
            return lax.dynamic_slice(total, (low, 0), (own_rows, total.shape[1])).astype(BF16)

        return (rows_of(0), jnp.stack([rows_of(1), rows_of(3)]), rows_of(2))

    def unstack_rows(total):
        return jnp.concatenate(
            [total[k * own_rows : (k + 1) * own_rows] for k in range(4)], axis=1
        ).astype(BF16)

    def cross_backward(queries, text, grads, skip):
        return by_image(
            functools.partial(cross_backward_kernel, rank_width, scale),
            [queries, text, grads],
            [(L, rank_width), (ctx, 2 * rank_width), (L, rank_width)],
            [(pair_rows, rank_width), (2 * images * ctx, 2 * rank_width)],
            [(L, rank_width), (ctx, 2 * rank_width)],
            5 * score_flops * ctx,
            skip,
        )

    from_x = pin(from_x)
    second_far = jnp.concatenate([from_x, pin(send(from_x, swap_core))])
    cgrad_far = back_project(second_far, w_cross_out).astype(BF16)
    cq_far, tkv_far = cross_backward(cross_far, text_kv, cgrad_far, 2 * images)
    two_grad = pin(back_project(cq_far, w_cross).astype(BF16))
    from_x = send_far(pair(two_grad))
    second_near = pin(second_near)
    cgrad_near = back_project(second_near, w_cross_out).astype(BF16)
    cq_near, tkv_near = cross_backward(cross_near, text_kv, cgrad_near, 0)
    two_grad = pair(pin(back_project(cq_near, w_cross)))
    from_core = pin(send(two_grad[1].astype(BF16), swap_core))
    (from_x,) = ring_with(from_x)
    cq_near, cq_far, tkv_near, tkv_far, second_far = pin(
        cq_near, cq_far, tkv_near, tkv_far, second_far
    )
    normed_two_grad = add_near(two_grad[0], from_core, from_x)
    rows_two, gain_cross_term, bias_cross_term = norm_backward(
        normed_two_grad, unit_two, inverse_two, g_cross
    )
    first_grad = second_grad + rows_two
    first_grad, gain_cross_term, bias_cross_term, first_low = pin(
        first_grad, gain_cross_term, bias_cross_term, first_grad.astype(BF16)
    )
    from_x = send(first_low, swap_x)
    first_near = join_near(first_low, pin(send(first_low, swap_core)))
    cmixed_all = jnp.concatenate([cmixed_near, cmixed_far])
    second_all = jnp.concatenate([second_near, second_far])
    cross_out_part = pin(outer_grad(cmixed_all, second_all).astype(BF16))
    two_all = jnp.concatenate([two_near, two_far])
    cq_all = jnp.concatenate([cq_near, cq_far])
    tkv_all = jnp.concatenate([tkv_near, tkv_far])
    cross_part = pin(outer_grad(two_all, cq_all).astype(BF16))
    (from_x,) = ring_with(from_x)
    tkv_all, first_near = pin(tkv_all, first_near)
    text_kv_part = pin(outer_grad(text_rows, tkv_all).astype(BF16))
    enter(
        reduce_task(
            "cross",
            text_kv_part.reshape(n_g, block_rows, 2 * rank_width),
            cross_part.reshape(n_g, block_rows, rank_width),
            cross_out_part.reshape(n_g, own_rows, width),
        )
    )
    sgrad_near = pin(back_project(first_near, w_out).astype(BF16))

    def self_backward(qkv, grads):
        return by_image(
            functools.partial(self_backward_kernel, rank_width, scale),
            [qkv, grads],
            [(L, 3 * rank_width), (L, rank_width)],
            [(pair_rows, 3 * rank_width)],
            [(L, 3 * rank_width)],
            5 * score_flops * L,
        )[0]

    qkv_grad_near = pin(self_backward(qkv_near, sgrad_near))
    ring()
    from_x = pin(from_x)
    first_far = jnp.concatenate([from_x, pin(send(from_x, swap_core))])
    sgrad_far = back_project(first_far, w_out).astype(BF16)
    qkv_grad_far = pin(self_backward(qkv_far, sgrad_far))
    ring()
    one_grad = pin(back_project(qkv_grad_far, w_qkv).astype(BF16))
    from_x = send_far(pair(one_grad))
    one_all = jnp.concatenate([one_near, one_far])
    qkv_grad_all = jnp.concatenate([qkv_grad_near, qkv_grad_far])
    qkv_part = pin(outer_grad(one_all, qkv_grad_all).astype(BF16))
    (from_x,) = ring_with(from_x)
    first_far, qkv_grad_near = pin(first_far, qkv_grad_near)
    mixed_all = jnp.concatenate([mixed_near, mixed_far])
    first_all = jnp.concatenate([first_near, first_far])
    out_part = pin(outer_grad(mixed_all, first_all).astype(BF16))
    enter(
        reduce_task(
            "self",
            qkv_part.reshape(n_g, block_rows, 3 * rank_width),
            out_part.reshape(n_g, own_rows, width),
        )
    )
    one_grad = pair(pin(back_project(qkv_grad_near, w_qkv)))
    from_core = pin(send(one_grad[1].astype(BF16), swap_core))
    normed_one_grad = add_near(one_grad[0], from_core, from_x)
    rows_one, gain_attn_term, bias_attn_term = norm_backward(
        normed_one_grad, unit_one, inverse_one, g_attn
    )
    start_grad = first_grad + rows_one
    tokens_grad = jnp.where(masked, 0.0, start_grad)
    embed_term = jnp.sum(jnp.where(masked, start_grad, 0.0), axis=0)
    tokens_grad, embed_term, gain_attn_term, bias_attn_term = pin(
        tokens_grad, embed_term, gain_attn_term, bias_attn_term
    )
    ring()

    activated_far, activated_near, tkv_all = pin(activated_far, activated_near, tkv_all)
    result_far = pin(product(activated_far, w_down).astype(BF16))
    from_x = send_far(pair(result_far))
    result_near = pair(pin(product(activated_near, w_down)))
    from_core = pin(send(result_near[1].astype(BF16), swap_core))
    (from_x,) = ring_with(from_x)
    tkv_all = pin(tkv_all)
    text_part = pin(back_project(tkv_all, w_text)).reshape(8, ctx // 2, width)
    output = pin((second + add_near(result_near[0], from_core, from_x)).astype(BF16))
    ring()
    text_own = jnp.stack([text_part[0], text_part[4]])
    text_far = [
        jnp.stack([text_part[a], text_part[b]]).astype(BF16) for a, b in ((5, 1), (2, 6), (7, 3))
    ]
    from_x = send_far([text_far[0], text_far[2]])
    from_core = pin(send(text_far[1], swap_core))
    in_sum, mlp_out_grad = pin(summed("in"), summed("down"))
    in_state = exchange_x(by_target(in_sum))
    text_sum = add_near(text_own, from_core, pin(from_x))
    in_state = exchange_core(in_state)
    ring()
    text_grad = pin(
        jnp.stack(
            [
                jnp.where(x == 1, text_sum[1], text_sum[0]),
                jnp.where(x == 1, text_sum[0], text_sum[1]),
            ]
        )
    )
    (mlp_in_grad,) = join_columns(*exchange_end(in_state), hidden_cut, 1)
    mlp_in_grad = pin(mlp_in_grad)

    cross_sum = summed("cross")
    cross_state = exchange_x(by_target(cross_sum[:, : 3 * rank_width]))
    cross_out_grad = send(unstack_rows(cross_sum[:, 3 * rank_width :]), from_ranks)
    cross_state = exchange_core(cross_state)
    cross_key_grad, cross_value_grad, cross_query_grad = join_columns(
        *exchange_end(cross_state), head_cut, 3
    )
    cross_query_grad, cross_key_grad, cross_value_grad, cross_out_grad = pin(
        cross_query_grad, cross_key_grad, cross_value_grad, cross_out_grad.astype(F32)
    )
    terms = jnp.stack(
        [
            embed_term,
            gain_attn_term,
            bias_attn_term,
            gain_cross_term,
            bias_cross_term,
            gain_mlp_term,
            bias_mlp_term,
            jnp.zeros_like(bias_mlp_term),
        ]
    )
    terms = terms.reshape(8, n, own_rows).transpose(1, 0, 2)
    for bit in reversed(range(bits)):
        upper = (me >> bit) & 1 == 1
        count = terms.shape[0] // 2
        keep = jnp.where(upper, terms[count:], terms[:count])
        away = jnp.where(upper, terms[:count], terms[count:])
        terms = keep + pin(send(away, [(i, i ^ (1 << bit)) for i in range(n)]))
    terms = terms[0]

    self_sum = summed("self")
    attn_out_grad = send(unstack_rows(self_sum[:, 3 * rank_width :]), from_ranks).astype(F32)
    qkv_state = exchange_core(exchange_x(by_target(self_sum[:, : 3 * rank_width])))
    attn_query_grad, attn_key_grad, attn_value_grad = join_columns(
        *exchange_end(qkv_state), head_cut, 3
    )

    return (
        output,
        tokens_grad,
        text_grad,
        terms[0],
        terms[1],
        terms[2],
        attn_query_grad,
        attn_key_grad,
        attn_value_grad,
        attn_out_grad,
        terms[3],
        terms[4],
        cross_query_grad,
        cross_key_grad,
        cross_value_grad,
        cross_out_grad,
        terms[5],
        terms[6],
        mlp_in_grad,
        mlp_out_grad,
    )


def solution(mesh):
    devices = mesh.devices.reshape(mesh.shape["dp"] // 2, 2, mesh.shape["text"])
    groups = jax.sharding.Mesh(devices, ("g", "core", "x"))
    spec_rows = P(AXES, None)
    spec_text = P(("g", "core"), "x", None)
    spec_vector = P(AXES)
    return jax.shard_map(
        functools.partial(on_device, groups.shape["g"]),
        mesh=groups,
        in_specs=(spec_rows, spec_vector, spec_text)
        + (spec_vector,) * 3
        + (spec_rows,) * 4
        + (spec_vector,) * 2
        + (spec_rows,) * 4
        + (spec_vector,) * 2
        + (spec_rows,) * 3,
        out_specs=(spec_rows, spec_rows, spec_text)
        + (spec_vector,) * 3
        + (spec_rows,) * 4
        + (spec_vector,) * 2
        + (spec_rows,) * 4
        + (spec_vector,) * 2
        + (spec_rows,) * 2,
        check_vma=False,
    )
```
